256 devices in a mesh: oct: 8 (over y, core), leaf: 32 (over z, x).
Axes of the slice: x: 4, y: 4, z: 8, core: 2. Of those that a mesh axis runs over, the one named last changes fastest.
Arguments:
- probes: bfloat16 [64, 1048576], P(None, ('oct', 'leaf')), may hold values from -6 to 6
- offsets: bfloat16 [3, 1048576], P(None, ('oct', 'leaf')), may hold values from 0 to 1
- leaf_basis: bfloat16 [131072, 512], P(('oct', 'leaf')), may hold values from -0.75 to 0.75
- dev_transfer: float32 [16384, 512], P(('oct', 'leaf')), may hold values from -0.25 to 0.25
- oct_transfer: float32 [16384, 64], P(('oct', 'leaf')), may hold values from -0.75 to 0.75
- near_list: int32 [2048, 5], P(('oct', 'leaf')), may hold values from 0 to 2047, as said below
- near_count: int32 [2048], P(('oct', 'leaf')), may hold values from 2 to 5, as said below
- leaf_far: int32 [2048, 4], P(('oct', 'leaf')), may hold values from 0 to 2047, as said below
- dev_far: int32 [256, 4], P(('oct', 'leaf')), may hold values from 0 to 255, as said below
- oct_far: int32 [8, 2], P('oct'), may hold values from 0 to 7, as said below
- leaf_skel: int32 [2048, 64], P(('oct', 'leaf')), may hold values from 0 to 511, as said below
- dev_skel: int32 [256, 64], P(('oct', 'leaf')), may hold values from 0 to 511, as said below
- oct_skel: int32 [8, 64], replicated, may hold values from 0 to 2047, as said below
Outputs:
- kernel_product: float32 [64, 1048576], P(None, ('oct', 'leaf'))
- derivative_product: float32 [64, 1048576], P(None, ('oct', 'leaf'))
The draws below stay inside these ranges and needn't reach their ends.
Inputs may be any that keep to these rules, and one draw needn't show every extreme that they name: `near_list`: slot 0 of a leaf's list is the leaf itself; every entry is a leaf at most 2 places away in Morton order. `near_count`: whole devices are busy: on some devices every leaf uses all 5 slots, elsewhere two to 4. `leaf_far`: every entry is a leaf 3 to 8 places away in Morton order. `dev_far`: every entry is another device node of the same region, distinct within a row. `oct_far`: entries are other regions, distinct within a row. `leaf_skel`: distinct within a row. `dev_skel`: distinct within a row. `oct_skel`: distinct within a row.
All inputs are finite; a program needn't handle non-finite values.
Results may differ from the reference program's by a relative error of at most 0.003.
Values may be sent and summed in bfloat16 or wider, within the bound.
A program may use at most 128 MiB of HBM per device.

```python
import math
import jax
import jax.numpy as jnp
from jax import lax

PROBES = 64
LEAF = 512
SKEL = 64
LEAVES_DEV = 8
NEAR_WIN = 2
FAR_LEAF = 4
FAR_DEV = 4
FAR_OCT = 2
NEAR_SLOTS = 5
DEV_NODES = 256
LEAVES = 2048
POINTS = 1048576
N_OCT = 8
N_LEAF = 32


def shuffled_rows(key, rows, values, keep):
    row_keys = jax.random.split(key, rows)
    return jax.vmap(lambda row_key: jax.random.permutation(row_key, values))(row_keys)[:, :keep]


def near_lists(key):
    leaf_ids = jnp.arange(LEAVES, dtype=jnp.int32)
    reach = jnp.arange(1, NEAR_WIN + 1, dtype=jnp.int32)
    candidates = jnp.concatenate([reach, -reach])
    shuffled = shuffled_rows(jax.random.fold_in(key, 11), LEAVES, candidates, 2 * NEAR_WIN)
    shifts = jnp.concatenate([jnp.zeros((LEAVES, 1), jnp.int32), shuffled], axis=1)
    forward = leaf_ids[:, None] + shifts
    partner = jnp.where((forward < 0) | (forward >= LEAVES), leaf_ids[:, None] - shifts, forward)
    devices = LEAVES // LEAVES_DEV
    heavy = jax.random.randint(jax.random.fold_in(key, 13), (devices,), 0, 4) == 0
    heavy = heavy.at[0].set(True)
    light = jax.random.randint(jax.random.fold_in(key, 12), (LEAVES,), 2, NEAR_SLOTS)
    counts = jnp.where(jnp.repeat(heavy, LEAVES_DEV), NEAR_SLOTS, light)
    return (partner.astype(jnp.int32), counts.astype(jnp.int32))


def draw_near_list(key, part):
    return near_lists(key)[0]


def draw_near_count(key, part):
    return near_lists(key)[1]


def draw_leaf_far(key, part):
    key = jax.random.fold_in(key, 21)
    leaf_ids = jnp.arange(LEAVES, dtype=jnp.int32)
    reach = jnp.arange(NEAR_WIN + 1, LEAVES_DEV + 1, dtype=jnp.int32)
    candidates = jnp.concatenate([reach, -reach])
    shifts = shuffled_rows(key, LEAVES, candidates, FAR_LEAF)
    forward = leaf_ids[:, None] + shifts
    partner = jnp.where((forward < 0) | (forward >= LEAVES), leaf_ids[:, None] - shifts, forward)
    return partner.astype(jnp.int32)


def draw_dev_far(key, part):
    key = jax.random.fold_in(key, 31)
    nodes = jnp.arange(N_OCT * N_LEAF, dtype=jnp.int32)
    reach = jnp.arange(2, N_LEAF - 1, dtype=jnp.int32)
    shifts = shuffled_rows(key, N_OCT * N_LEAF, reach, FAR_DEV)
    within = nodes % N_LEAF
    return ((nodes - within)[:, None] + (within[:, None] + shifts) % N_LEAF).astype(jnp.int32)


def draw_oct_far(key, part):
    key = jax.random.fold_in(key, 41)
    regions = jnp.arange(N_OCT, dtype=jnp.int32)
    reach = jnp.arange(1, N_OCT, dtype=jnp.int32)
    shifts = shuffled_rows(key, N_OCT, reach, FAR_OCT)
    return ((regions[:, None] + shifts) % N_OCT).astype(jnp.int32)


def draw_leaf_skel(key, part):
    key = jax.random.fold_in(key, 51)
    return shuffled_rows(key, LEAVES, jnp.arange(LEAF, dtype=jnp.int32), SKEL).astype(jnp.int32)


def draw_dev_skel(key, part):
    key = jax.random.fold_in(key, 61)
    return shuffled_rows(key, N_OCT * N_LEAF, jnp.arange(LEAVES_DEV * SKEL, dtype=jnp.int32), SKEL).astype(jnp.int32)


def draw_oct_skel(key, part):
    key = jax.random.fold_in(key, 71)
    return shuffled_rows(key, N_OCT, jnp.arange(N_LEAF * SKEL, dtype=jnp.int32), SKEL).astype(jnp.int32)


def steps_of(stream_key, shape, pieces, least, top_value):
    loudness = 1.0
    for position, shards_of in pieces:
        draws = jax.random.uniform(jax.random.fold_in(jax.random.fold_in(stream_key, 6), position), (shards_of,), jnp.float32, least / len(pieces), top_value / len(pieces))
        loudness = loudness * jnp.repeat(jnp.exp(draws), shape[position] // shards_of).reshape((-1,) + (1,) * (len(shape) - 1 - position))
    return loudness


def normal_values(key, extent, deviation, bound, shards=(), held_as=jnp.bfloat16):
    gain = steps_of(key, extent, shards, -0.22, 0.18) if shards else 1.0
    values = jax.random.normal(key, extent, jnp.float32) * deviation * gain
    return jnp.minimum(jnp.maximum(values, -bound), bound).astype(held_as)


def setup_inputs(seed: int = 0) -> dict:
    seeds = jax.random.split(jax.random.key(seed), 14)
    probes = normal_values(seeds[0], (PROBES, POINTS), 1.0, 6.0, ((1, 256),))
    offsets = jnp.clip(1.0 * jax.random.uniform(seeds[1], (3, POINTS), jnp.float32) ** steps_of(seeds[1], (3, POINTS), ((1, 256),), -0.2, 0.2), 0.0, 1.0).astype(jnp.bfloat16)
    leaf_basis = normal_values(seeds[2], (LEAVES * SKEL, LEAF), SKEL ** -0.5, 0.75, ((0, 256),))
    dev_transfer = normal_values(seeds[3], (DEV_NODES * SKEL, LEAVES_DEV * SKEL), (LEAVES_DEV * SKEL) ** -0.5, 0.25, ((0, 256),), jnp.float32)
    oct_transfer = normal_values(seeds[4], (DEV_NODES * SKEL, SKEL), SKEL ** -0.5, 0.75, ((0, 256),), jnp.float32)
    near_list = draw_near_list(jax.random.fold_in(seeds[13], 71), 0)
    near_count = draw_near_count(jax.random.fold_in(seeds[13], 71), 0)
    leaf_far = draw_leaf_far(jax.random.fold_in(seeds[13], 71), 0)
    dev_far = draw_dev_far(jax.random.fold_in(seeds[13], 71), 0)
    oct_far = draw_oct_far(jax.random.fold_in(seeds[13], 71), 0)
    leaf_skel = draw_leaf_skel(jax.random.fold_in(seeds[13], 71), 0)
    dev_skel = draw_dev_skel(jax.random.fold_in(seeds[13], 71), 0)
    oct_skel = draw_oct_skel(jax.random.fold_in(seeds[13], 71), 0)
    return {"probes": probes, "offsets": offsets, "leaf_basis": leaf_basis, "dev_transfer": dev_transfer, "oct_transfer": oct_transfer, "near_list": near_list, "near_count": near_count, "leaf_far": leaf_far, "dev_far": dev_far, "oct_far": oct_far, "leaf_skel": leaf_skel, "dev_skel": dev_skel, "oct_skel": oct_skel}


broad_scale = 6.0
sharp_scale = 0.25
broad_var = 0.08
sharp_var = 0.1
broad_rate = math.sqrt(3.0) / broad_scale
sharp_rate = math.sqrt(3.0) / sharp_scale
highest = lax.Precision.HIGHEST

def box_anchor(leaf_index):
    corners = []
    for coord_axis in range(3):
        summed = jnp.zeros(leaf_index.shape, jnp.int32)
        for bit_index in range(10):
            summed = summed + (leaf_index >> 3 * bit_index + coord_axis & 1) * (1 << bit_index)
        corners.append(summed)
    return jnp.stack(corners).astype(jnp.float32)

def matern_pair(target, source):
    squared = jnp.zeros((target.shape[1], source.shape[1]), jnp.float32)
    for coord_axis in range(3):
        between = target[coord_axis][:, None] - source[coord_axis][None, :]
        squared = squared + between * between
    distance = jnp.sqrt(squared)
    wide_scaled = broad_rate * distance
    narrow_scaled = sharp_rate * distance
    wide_fading = jnp.exp(-wide_scaled)
    narrow_fading = jnp.exp(-narrow_scaled)
    kernel_value = broad_var * (1.0 + wide_scaled) * wide_fading + sharp_var * (1.0 + narrow_scaled) * narrow_fading
    kernel_slope = broad_var * wide_scaled * wide_scaled * wide_fading + sharp_var * narrow_scaled * narrow_scaled * narrow_fading
    return (kernel_value, kernel_slope)

def couple(target, source, charges):
    kernel_value, kernel_slope = matern_pair(target, source)
    return jnp.stack([jnp.dot(kernel_value, charges, precision=highest), jnp.dot(kernel_slope, charges, precision=highest)])

def sum_couple(target, sources, charges):
    return lax.optimization_barrier(jnp.sum(jax.vmap(couple, (None, 0, 0))(target, sources, charges), axis=0))

def near_term(target_pos, source_pos, source_probes):
    kernel_value, kernel_slope = matern_pair(source_pos, target_pos)
    first = jnp.dot(source_probes, kernel_value.astype(jnp.bfloat16), preferred_element_type=jnp.float32)
    second = jnp.dot(source_probes, kernel_slope.astype(jnp.bfloat16), preferred_element_type=jnp.float32)
    return jnp.stack([first, second])

def skipped(target_pos, source_pos, source_probes):
    return jnp.zeros((2, source_probes.shape[0], target_pos.shape[1]), jnp.float32)

def reference(probes, offsets, leaf_basis, dev_transfer, oct_transfer, near_list, near_count, leaf_far, dev_far, oct_far, leaf_skel, dev_skel, oct_skel):
    leaf_ids = jnp.arange(LEAVES, dtype=jnp.int32)
    positions = box_anchor(leaf_ids)[:, :, None] + offsets.reshape(3, LEAVES, LEAF).astype(jnp.float32)
    leaf_pos = jnp.take_along_axis(positions, leaf_skel[None], axis=2)
    dev_flat = leaf_pos.reshape(3, DEV_NODES, LEAVES_DEV * SKEL)
    dev_pos = jnp.take_along_axis(dev_flat, dev_skel[None], axis=2)
    oct_flat = dev_pos.reshape(3, N_OCT, N_LEAF * SKEL)
    oct_pos = jnp.take_along_axis(oct_flat, oct_skel[None], axis=2)
    leaf_pos_t = jnp.transpose(leaf_pos, (1, 0, 2))
    dev_pos_t = jnp.transpose(dev_pos, (1, 0, 2))
    oct_pos_t = jnp.transpose(oct_pos, (1, 0, 2))
    leaf_bases = leaf_basis.reshape(LEAVES, SKEL, LEAF)
    q_leaf = jnp.einsum('lsn,pln->lsp', leaf_bases.astype(jnp.float32), probes.reshape(PROBES, LEAVES, LEAF).astype(jnp.float32), precision=highest)
    dev_blocks = dev_transfer.reshape(DEV_NODES, SKEL, LEAVES_DEV * SKEL)
    oct_blocks = oct_transfer.reshape(DEV_NODES, SKEL, SKEL)
    q_dev = jnp.einsum('dsm,dmp->dsp', dev_blocks, q_leaf.reshape(DEV_NODES, LEAVES_DEV * SKEL, PROBES), precision=highest)
    upward = jnp.einsum('dst,dtp->dsp', oct_blocks, q_dev, precision=highest)
    q_oct = lax.optimization_barrier(jnp.sum(upward.reshape(N_OCT, N_LEAF, SKEL, PROBES), axis=1))
    far_oct = jax.vmap(lambda target, partner: sum_couple(target, oct_pos_t[partner], q_oct[partner]))(oct_pos_t, oct_far)
    far_dev = jax.vmap(lambda target, partner: sum_couple(target, dev_pos_t[partner], q_dev[partner]))(dev_pos_t, dev_far)
    dev_region = jnp.arange(DEV_NODES, dtype=jnp.int32) // N_LEAF
    down_dev = jnp.einsum('dst,dksp->dktp', oct_blocks, far_oct[dev_region], precision=highest) + far_dev
    far_leaf = jax.vmap(lambda target, partner: sum_couple(target, leaf_pos_t[partner], q_leaf[partner]))(leaf_pos_t, leaf_far)
    down_cat = jnp.einsum('dsm,dksp->dkmp', dev_blocks, down_dev, precision=highest)
    down_cat = jnp.transpose(down_cat.reshape(DEV_NODES, 2, LEAVES_DEV, SKEL, PROBES), (0, 2, 1, 3, 4))
    down_leaf = (down_cat.reshape(LEAVES, 2, SKEL, PROBES) + far_leaf).astype(jnp.bfloat16)
    far_out = jnp.einsum('lksp,lsn->kpln', down_leaf.astype(jnp.float32), leaf_bases.astype(jnp.float32), precision=highest).reshape(2, PROBES, POINTS)

    def near_leaf(leaf_slot, totals):
        slot_now = jnp.asarray(leaf_slot).astype(jnp.int32)
        target_pos = lax.dynamic_index_in_dim(positions, slot_now, 1, keepdims=False)
        summed = jnp.zeros((2, PROBES, LEAF), jnp.float32)
        for slot_index in range(NEAR_SLOTS):
            source = near_list[slot_now, slot_index].astype(jnp.int32)
            source_pos = lax.dynamic_index_in_dim(positions, source, 1, keepdims=False)
            source_probes = lax.dynamic_slice_in_dim(probes, source * LEAF, LEAF, 1)
            summed = summed + lax.cond(slot_index < near_count[slot_now], near_term, skipped, target_pos, source_pos, source_probes)
        return lax.dynamic_update_slice_in_dim(totals, summed, slot_now * LEAF, 2)
    near_out = lax.fori_loop(0, LEAVES, near_leaf, jnp.zeros((2, PROBES, POINTS), jnp.float32))
    result = near_out + far_out
    return (result[0], result[1])
```

```python
import functools
import math

import jax
import jax.numpy as jnp
from jax import lax
from jax.experimental import pallas as pl
from jax.experimental.pallas import tpu as pltpu
from jax.sharding import PartitionSpec as P

LEAF = 512
SKEL = 64
PROBES = 64
LEAVES = 8
WIN = 2
EXT = LEAVES + 2 * WIN
WIDE = 3 * LEAVES
RED = 9
FEAT = 64

MESH = pl.DeviceIdType.MESH
f32 = jnp.float32
bf16 = jnp.bfloat16
LOG2E = math.log2(math.e)
NN = (((1,), (0,)), ((), ()))
NT = (((1,), (1,)), ((), ()))


def dot(a, b, dims=NN):
    return lax.dot_general(a, b, dims, preferred_element_type=f32)


def halves(v):
    high = v.astype(bf16)
    return high, (v - high.astype(f32)).astype(bf16)


def dot3(a, b, dims=NN):
    ah, al = halves(a)
    bh, bl = halves(b)
    return dot(ah, bh, dims) + (dot(ah, bl, dims) + dot(al, bh, dims))


def split3(v):
    high = v.astype(bf16).astype(f32)
    rest = v - high
    mid = rest.astype(bf16).astype(f32)
    return high, mid, (rest - mid).astype(bf16).astype(f32)


def matern(w):
    w = jnp.maximum(w, 1e-30)
    t = w * lax.rsqrt(w)
    wide = jnp.exp2(t * (-LOG2E))
    cube = wide * wide * wide
    six = cube * cube
    twelve = six * six
    sharp = twelve * twelve
    wide = 0.08 * wide
    value = (wide + 0.1 * sharp) + t * (wide + 2.4 * sharp)
    slope = w * (wide + 57.6 * sharp)
    return value, slope


def box_corner(leaf):
    corner = []
    for axis in range(3):
        total = 0
        for bit in range(4):
            total = total + ((leaf >> (3 * bit + axis)) & 1) * (1 << bit)
        corner.append(total)
    return corner


def rows_of(corner, shape):
    row = lax.broadcasted_iota(jnp.int32, shape, 0)
    x, y, z = [jnp.asarray(c, jnp.int32).astype(f32) for c in corner]
    return jnp.where(row == 0, x, jnp.where(row == 1, y, jnp.where(row == 2, z, 0.0)))


def inside(index, count):
    return jnp.minimum(jnp.maximum(index, 0), count - 1)


def stacked(v):
    return jnp.concatenate([v[:, :SKEL], v[:, SKEL:]], axis=0)


def far_tile(columns, source):
    w = None
    for axis in range(3):
        gap = columns[axis] - source[axis : axis + 1, :]
        w = gap * gap if w is None else w + gap * gap
    value, slope = matern(w * (1.0 / 12.0))
    return jnp.concatenate([value, slope], axis=0)


def kernel(
    n_oct,
    n_leaf,
    probes,
    offsets,
    basis,
    dev_transfer,
    oct_transfer,
    leaf_skel,
    dev_skel,
    oct_skel,
    near_list,
    near_count,
    leaf_far,
    dev_far,
    oct_far,
    out_value,
    out_slope,
    pext,
    oext,
    wq,
    wsk,
    ag,
    tiles,
    gathered,
    regions,
    chosen,
    spread,
    feat_f,
    feat_g,
    kv0,
    ks0,
    kv1,
    ks1,
    acc,
    columns,
    far_sum,
    halo_send,
    halo_recv,
    ag_send,
    ag_recv,
    red_send,
    red_recv,
    oct_send,
    oct_recv,
    spread_send,
    spread_recv,
):
    o = lax.axis_index("oct")
    me = lax.axis_index("leaf")
    flat = o * n_leaf + me
    devices = n_oct * n_leaf
    right = lax.rem(flat + 1, devices)
    left = lax.rem(flat + devices - 1, devices)
    right_id = (right // n_leaf, lax.rem(right, n_leaf))
    left_id = (left // n_leaf, lax.rem(left, n_leaf))
    first = flat * LEAVES

    def in_region(k):
        return lax.rem(me + k, n_leaf)

    def across(k):
        return lax.rem(o + k, n_oct)

    barrier = pltpu.get_barrier_semaphore()

    def greet(device):
        pl.semaphore_signal(barrier, inc=1, device_id=device, device_id_type=MESH)

    greet(right_id)
    greet(left_id)

    def greet_region(k, _):
        greet((o, in_region(k)))
        return 0

    lax.fori_loop(1, n_leaf, greet_region, 0)

    def greet_across(k, _):
        greet((across(k), me))
        return 0

    lax.fori_loop(1, n_oct, greet_across, 0)

    base = box_corner(first)
    row512 = lax.broadcasted_iota(jnp.int32, (LEAF, SKEL), 0)
    charges, picked, corners = [], [], []
    for leaf in range(LEAVES):
        span = slice(leaf * LEAF, (leaf + 1) * LEAF)
        pext[WIN + leaf] = probes[:, span]
        own = jnp.concatenate([offsets[:, span].astype(f32), jnp.zeros((5, LEAF), f32)], axis=0)
        oext[WIN + leaf] = own
        one_hot = jnp.where(row512 == leaf_skel[leaf : leaf + 1, :], 1.0, 0.0).astype(bf16)
        picked.append(dot(own.astype(bf16), one_hot))
        corner = [base[0] + (leaf & 1), base[1] + (leaf >> 1 & 1), base[2] + (leaf >> 2 & 1)]
        corners.append(rows_of(corner, (8, SKEL)))
        wsk[LEAVES + leaf] = picked[-1] + corners[-1]
        charge = dot(pext[WIN + leaf], basis[leaf * SKEL : (leaf + 1) * SKEL, :], NT)
        charges.append(charge)
        wq[LEAVES + leaf] = jnp.concatenate(halves(charge), axis=1)
    q_dev = dot3(jnp.concatenate(charges, axis=1), dev_transfer[...], NT)
    upward = dot3(q_dev, oct_transfer[...], NT)
    both = jnp.concatenate(
        [jnp.concatenate(picked, axis=1), jnp.concatenate(corners, axis=1)], axis=0
    ).astype(bf16)
    one_hot = jnp.where(row512 == dev_skel[...], 1.0, 0.0).astype(bf16)
    dev_both = dot(both, one_hot)
    dev_pos = dev_both[:8] + dev_both[8:]
    ag[me] = jnp.concatenate(
        [q_dev, jnp.concatenate([dev_both, jnp.zeros((PROBES - 16, SKEL), f32)], axis=0)], axis=1
    ).astype(bf16)
    wanted = oct_skel[pl.ds(o, 1), :] - me * SKEL
    row64 = lax.broadcasted_iota(jnp.int32, (SKEL, SKEL), 0)
    one_hot = jnp.where(row64 == wanted, 1.0, 0.0).astype(bf16)
    oct_both = dot(dev_both.astype(bf16), one_hot)
    blank = jnp.zeros((8, SKEL), f32)
    for t in range(RED - 1):
        tiles[t] = jnp.concatenate([upward[8 * t : 8 * t + 8], blank], axis=1)
    tiles[RED - 1] = jnp.concatenate([oct_both[:8] + oct_both[8:], blank], axis=1)

    pl.semaphore_wait(barrier, n_leaf - 1 + n_oct - 1 + 2)

    def copy(src, dst, send, recv, device):
        return pltpu.make_async_remote_copy(
            src_ref=src,
            dst_ref=dst,
            send_sem=send,
            recv_sem=recv,
            device_id=device,
            device_id_type=MESH,
        )

    def reduce_copy(t, slot):
        return copy(
            tiles.at[t], gathered.at[slot], red_send.at[t], red_recv.at[slot], (o, t)
        )

    for t in range(RED):

        @pl.when(me != t)
        def _():
            reduce_copy(t, me).start()

    @pl.when(me < RED)
    def _():
        gathered[me] = tiles[me]

    own = slice(LEAVES, 2 * LEAVES)
    halo = [
        copy(pext.at[WIN : 2 * WIN], pext.at[WIN + LEAVES : EXT], halo_send.at[0], halo_recv.at[0], left_id),
        copy(oext.at[WIN : 2 * WIN], oext.at[WIN + LEAVES : EXT], halo_send.at[1], halo_recv.at[1], left_id),
        copy(pext.at[LEAVES : LEAVES + WIN], pext.at[0:WIN], halo_send.at[2], halo_recv.at[2], right_id),
        copy(oext.at[LEAVES : LEAVES + WIN], oext.at[0:WIN], halo_send.at[3], halo_recv.at[3], right_id),
        copy(wq.at[own], wq.at[2 * LEAVES : WIDE], halo_send.at[4], halo_recv.at[4], left_id),
        copy(wsk.at[own], wsk.at[2 * LEAVES : WIDE], halo_send.at[5], halo_recv.at[5], left_id),
        copy(wq.at[own], wq.at[0:LEAVES], halo_send.at[6], halo_recv.at[6], right_id),
        copy(wsk.at[own], wsk.at[0:LEAVES], halo_send.at[7], halo_recv.at[7], right_id),
    ]
    for piece in halo:
        piece.start()

    def gather_copy(peer, slot):
        return copy(ag.at[me], ag.at[slot], ag_send.at[peer], ag_recv.at[slot], (o, peer))

    def gather_start(k, _):
        gather_copy(in_region(k), me).start()
        return 0

    lax.fori_loop(1, n_leaf, gather_start, 0)

    row8 = lax.broadcasted_iota(jnp.int32, (8, LEAF), 0)

    def features(e, corner):
        off = oext[e]
        anchor = rows_of(corner, (8, LEAF))
        pos = off + anchor
        norm = split3(jnp.sum(pos * pos, axis=0, keepdims=True) * (1.0 / 12.0))
        parts = split3(pos * (-1.0 / 6.0))

        def mixed(at):
            v = jnp.zeros((8, LEAF), f32)
            for i in range(3):
                v = jnp.where(row8 == at + i, norm[i], v)
            return jnp.where((row8 >= 3 - at) & (row8 < 6 - at), 1.0, v)

        pad = jnp.zeros((8, LEAF), f32)
        rows_f = jnp.concatenate([*parts, *parts, mixed(0), pad], axis=0)
        feat_f[e] = jnp.transpose(rows_f).astype(bf16)
        rows_g = jnp.concatenate([anchor] * 3 + [off] * 3 + [mixed(3), pad], axis=0)
        feat_g[e] = rows_g.astype(bf16)

    for leaf in range(LEAVES):
        features(WIN + leaf, [leaf & 1, leaf >> 1 & 1, leaf >> 2 & 1])
    for e in range(EXT):
        acc[e] = jnp.zeros((2, PROBES, LEAF), f32)

    def uses(target, source):
        leaf = lax.rem(target + LEAVES - WIN, LEAVES)
        wanted_leaf = first + source - WIN
        count = near_count[leaf]
        total = jnp.float32(0.0)
        for s in range(near_list.shape[1]):
            hit = (near_list[leaf, s] == wanted_leaf) & (s < count)
            total = total + jnp.where(hit, jnp.float32(1.0), jnp.float32(0.0))
        return total

    def tile(a, b, kv, ks, rows, cols):
        value, slope = matern(dot(feat_f[a, rows, :], feat_g[b, :, cols]))
        kv[rows, cols] = value.astype(bf16)
        ks[rows, cols] = slope.astype(bf16)

    def interleave(first_ops, second_ops):
        done = 0
        for i, op in enumerate(first_ops):
            op()
            upto = (i + 1) * len(second_ops) // len(first_ops)
            for q in range(done, upto):
                second_ops[q]()
            done = upto

    def pipe(n, make, use, between=lambda k: None):
        bufs = ((kv0, ks0), (kv1, ks1))
        for op in make(0, *bufs[0]):
            op()
        steps = (n - 1) // 2

        def body(k, _):
            between(k)
            interleave(make(2 * k + 1, *bufs[1]), use(2 * k, *bufs[0]))
            interleave(make(2 * k + 2, *bufs[0]), use(2 * k + 1, *bufs[1]))
            return 0

        lax.fori_loop(0, steps, body, 0)
        if n % 2:
            for op in use(n - 1, *bufs[0]):
                op()
        else:
            interleave(make(n - 1, *bufs[1]), use(n - 2, *bufs[0]))
            for op in use(n - 1, *bufs[1]):
                op()

    half = LEAF // 2
    low, high, full = slice(0, half), slice(half, LEAF), slice(0, LEAF)

    def self_make(i, kv, ks):
        e = i + WIN
        ops = []
        for r in range(0, LEAF, 64):
            cols = full if r < half else high
            ops.append(lambda r=r, cols=cols: tile(e, e, kv, ks, slice(r, r + 64), cols))
        return ops

    def self_use(i, kv, ks):
        e = i + WIN
        c = uses(e, e)
        ops = []
        for m, k in enumerate((kv, ks)):

            def upper(m=m, k=k):
                acc[e, m] = c * dot(pext[e, :, low], k[low, :])

            def corner(m=m, k=k):
                acc[e, m, :, high] += c * dot(pext[e, :, high], k[high, high])

            def lower(m=m, k=k):
                acc[e, m, :, low] += c * dot(pext[e, :, high], k[low, high], NT)

            ops += [upper, corner, lower]
        return ops

    pipe(LEAVES, self_make, self_use)

    for piece in halo:
        piece.wait_recv()
    for e in list(range(WIN)) + list(range(WIN + LEAVES, EXT)):
        leaf = lax.rem(first + devices * LEAVES + e - WIN, devices * LEAVES)
        there = box_corner(leaf)
        features(e, [there[i] - base[i] for i in range(3)])

    def pair(i):
        s = (i + 1) // 10
        a = i + 1 - 10 * s
        return a, a + 1 + s

    def pair_make(i, kv, ks):
        a, b = pair(i)
        return [
            lambda r=r: tile(a, b, kv, ks, slice(r, r + 64), full) for r in range(0, LEAF, 64)
        ]

    def pair_use(i, kv, ks):
        a, b = pair(i)
        to_b = uses(b, a)
        to_a = uses(a, b)
        ops = []
        for m, k in enumerate((kv, ks)):
            for span in (low, high):

                def forward(m=m, k=k, span=span):
                    acc[b, m, :, span] += to_b * dot(pext[a], k[:, span])

                def back(m=m, k=k, span=span):
                    acc[a, m, :, span] += to_a * dot(pext[b], k[span, :], NT)

                ops += [forward, back]
        return ops

    def oct_copy(k, slot):
        return copy(
            tiles.at[0], regions.at[slot], oct_send.at[k], oct_recv.at[slot], (across(k), me)
        )

    def spread_copy(peer, slot):
        return copy(chosen, spread.at[slot], spread_send.at[peer], spread_recv.at[slot], (o, peer))

    def each(lo, hi, fn):
        def step(k, _):
            fn(k)
            return 0

        lax.fori_loop(lo, hi, step, 0)

    def sum_region():
        @pl.when(me < RED)
        def _():
            each(1, n_leaf, lambda k: reduce_copy(0, in_region(k)).wait_recv())
            for t in range(RED):

                @pl.when(me != t)
                def _():
                    reduce_copy(t, me).wait_send()

            total = jnp.sum(gathered[...], axis=0)
            regions[o] = total
            tiles[0] = total
            each(1, n_oct, lambda k: oct_copy(k, o).start())

    def spread_regions():
        @pl.when(me < RED)
        def _():
            each(1, n_oct, lambda k: oct_copy(k, across(k)).wait_recv())
            one, two = [regions[inside(oct_far[0, i], n_oct)] for i in range(2)]
            message = [jnp.concatenate([one[:, :SKEL], two[:, :SKEL]], axis=1), regions[o]]
            for m in range(2):
                chosen[m] = message[m]
                spread[me, m] = message[m]
            each(1, n_leaf, lambda k: spread_copy(in_region(k), me).start())

    def between(k):
        pl.when(k == 1)(sum_region)
        pl.when(k == 4)(spread_regions)

    pipe(19, pair_make, pair_use, between)

    upright = jnp.concatenate(
        [wsk[LEAVES + leaf] for leaf in range(LEAVES)] + [dev_pos] + [blank] * 7, axis=0
    )
    upright = jnp.transpose(upright)
    wide = (SKEL, 2 * SKEL)
    for leaf in range(LEAVES + 1):
        for axis in range(3):
            at = 8 * leaf + axis
            columns[leaf, axis] = jnp.broadcast_to(upright[:, at : at + 1], wide)

    def leaf_field(leaf, _):
        targets = [columns[leaf, axis] for axis in range(3)]
        total = jnp.zeros(wide, f32)
        for pairing in range(2):
            x = inside(leaf_far[leaf, 2 * pairing] - first + LEAVES, WIDE)
            y = inside(leaf_far[leaf, 2 * pairing + 1] - first + LEAVES, WIDE)
            source = jnp.concatenate([wsk[x], wsk[y]], axis=1)
            one, two = wq[x], wq[y]
            high = jnp.concatenate([one[:, :SKEL], two[:, :SKEL]], axis=1)
            rest = jnp.concatenate([one[:, SKEL:], two[:, SKEL:]], axis=1)
            tile_high, tile_rest = halves(far_tile(targets, source))
            total += dot(high, tile_high, NT) + (dot(rest, tile_high, NT) + dot(high, tile_rest, NT))
        far_sum[leaf] = total
        return 0

    lax.fori_loop(0, LEAVES, leaf_field, 0)

    each(1, n_leaf, lambda k: gather_copy(me, in_region(k)).wait_recv())
    targets = [columns[LEAVES, axis] for axis in range(3)]
    dev_sum = jnp.zeros(wide, f32)
    for pairing in range(2):
        pieces = [
            ag[inside(dev_far[0, 2 * pairing + i] - o * n_leaf, n_leaf)].astype(f32)
            for i in range(2)
        ]
        source = jnp.concatenate([v[:8, SKEL:] + v[8:16, SKEL:] for v in pieces], axis=1)
        charge = jnp.concatenate([v[:, :SKEL] for v in pieces], axis=1)
        dev_sum += dot3(charge, far_tile(targets, source), NT)

    for t in range(RED):

        @pl.when(me != t)
        def _():
            spread_copy(t, t).wait_recv()

    charge = spread[0 : RED - 1, 0].reshape(PROBES, 2 * SKEL)
    source = spread[RED - 1, 0]
    upright = jnp.transpose(
        jnp.concatenate([spread[RED - 1, 1], jnp.zeros((120, 2 * SKEL), f32)], axis=0)
    )
    targets = [upright[:SKEL, axis : axis + 1] for axis in range(3)]
    oct_sum = dot3(charge, far_tile(targets, source), NT)
    down_dev = dot3(stacked(oct_sum), oct_transfer[...]) + stacked(dev_sum)
    down = dot3(down_dev, dev_transfer[...])
    for leaf in range(LEAVES):
        span = slice(leaf * LEAF, (leaf + 1) * LEAF)
        cols = slice(leaf * SKEL, (leaf + 1) * SKEL)
        mine = (down[:, cols] + stacked(far_sum[leaf])).astype(bf16)
        field = dot(mine, basis[cols, :])
        out_value[:, span] = acc[WIN + leaf, 0] + field[:PROBES]
        out_slope[:, span] = acc[WIN + leaf, 1] + field[PROBES:]

    for piece in halo:
        piece.wait_send()
    each(1, n_leaf, lambda k: gather_copy(in_region(k), me).wait_send())

    @pl.when(me < RED)
    def _():
        each(1, n_oct, lambda k: oct_copy(k, o).wait_send())
        each(1, n_leaf, lambda k: spread_copy(in_region(k), me).wait_send())

    @pl.when(me >= RED)
    def _():
        for t in range(RED):
            reduce_copy(t, me).wait_send()


def body(n_oct, n_leaf, *args):
    (
        probes,
        offsets,
        leaf_basis,
        dev_transfer,
        oct_transfer,
        near_list,
        near_count,
        leaf_far,
        dev_far,
        oct_far,
        leaf_skel,
        dev_skel,
        oct_skel,
    ) = args
    vmem = pl.BlockSpec(memory_space=pltpu.VMEM)
    smem = pl.BlockSpec(memory_space=pltpu.SMEM)
    points = probes.shape[1]
    dma = pltpu.SemaphoreType.DMA
    out = jax.ShapeDtypeStruct((PROBES, points), f32)
    return pl.pallas_call(
        functools.partial(kernel, n_oct, n_leaf),
        out_shape=(out, out),
        in_specs=[vmem] * 8 + [smem] * 5,
        out_specs=(vmem, vmem),
        scratch_shapes=[
            pltpu.VMEM((EXT, PROBES, LEAF), bf16),
            pltpu.VMEM((EXT, 8, LEAF), f32),
            pltpu.VMEM((WIDE, PROBES, 2 * SKEL), bf16),
            pltpu.VMEM((WIDE, 8, SKEL), f32),
            pltpu.VMEM((n_leaf, PROBES, 2 * SKEL), bf16),
            pltpu.VMEM((RED, 8, 2 * SKEL), f32),
            pltpu.VMEM((n_leaf, 8, 2 * SKEL), f32),
            pltpu.VMEM((n_oct, 8, 2 * SKEL), f32),
            pltpu.VMEM((2, 8, 2 * SKEL), f32),
            pltpu.VMEM((RED, 2, 8, 2 * SKEL), f32),
            pltpu.VMEM((EXT, LEAF, FEAT), bf16),
            pltpu.VMEM((EXT, FEAT, LEAF), bf16),
            pltpu.VMEM((LEAF, LEAF), bf16),
            pltpu.VMEM((LEAF, LEAF), bf16),
            pltpu.VMEM((LEAF, LEAF), bf16),
            pltpu.VMEM((LEAF, LEAF), bf16),
            pltpu.VMEM((EXT, 2, PROBES, LEAF), f32),
            pltpu.VMEM((LEAVES + 1, 3, SKEL, 2 * SKEL), f32),
            pltpu.VMEM((LEAVES, PROBES, 2 * SKEL), f32),
            dma((8,)),
            dma((8,)),
            dma((n_leaf,)),
            dma((n_leaf,)),
            dma((RED,)),
            dma((n_leaf,)),
            dma((n_oct,)),
            dma((n_oct,)),
            dma((n_leaf,)),
            dma((n_leaf,)),
        ],
        compiler_params=pltpu.CompilerParams(
            collective_id=0, has_side_effects=True, vmem_limit_bytes=48 * 2**20
        ),
    )(
        probes,
        offsets,
        leaf_basis,
        dev_transfer,
        oct_transfer,
        leaf_skel,
        dev_skel,
        oct_skel,
        near_list,
        near_count,
        leaf_far,
        dev_far,
        oct_far,
    )


def solution(mesh):
    return jax.shard_map(
        functools.partial(body, mesh.shape["oct"], mesh.shape["leaf"]),
        mesh=mesh,
        in_specs=(
            P(None, ("oct", "leaf")),
            P(None, ("oct", "leaf")),
            P(("oct", "leaf"), None),
            P(("oct", "leaf"), None),
            P(("oct", "leaf"), None),
            P(("oct", "leaf"), None),
            P(("oct", "leaf")),
            P(("oct", "leaf"), None),
            P(("oct", "leaf"), None),
            P("oct", None),
            P(("oct", "leaf"), None),
            P(("oct", "leaf"), None),
            P(),
        ),
        out_specs=(P(None, ("oct", "leaf")), P(None, ("oct", "leaf"))),
        check_vma=False,
    )
```

```python
import functools
import math

import jax
import jax.numpy as jnp
from jax import lax
from jax.experimental import pallas as pl
from jax.experimental.pallas import tpu as pltpu
from jax.sharding import PartitionSpec as P

LEAF = 512
SKEL = 64
PROBES = 64
LEAVES = 8
WIN = 2
EXT = LEAVES + 2 * WIN
WIDE = 3 * LEAVES
RED = 9
FEAT = 64

MESH = pl.DeviceIdType.MESH
f32 = jnp.float32
bf16 = jnp.bfloat16
LOG2E = math.log2(math.e)
NN = (((1,), (0,)), ((), ()))
NT = (((1,), (1,)), ((), ()))


def dot(a, b, dims=NN):
    return lax.dot_general(a, b, dims, preferred_element_type=f32)


def halves(v):
    high = v.astype(bf16)
    return high, (v - high.astype(f32)).astype(bf16)


def dot3(a, b, dims=NN):
    ah, al = halves(a)
    bh, bl = halves(b)
    return dot(ah, bh, dims) + (dot(ah, bl, dims) + dot(al, bh, dims))


def split3(v):
    high = v.astype(bf16).astype(f32)
    rest = v - high
    mid = rest.astype(bf16).astype(f32)
    return high, mid, (rest - mid).astype(bf16).astype(f32)


def matern(w):
    w = jnp.maximum(w, 1e-30)
    t = w * lax.rsqrt(w)
    wide = jnp.exp2(t * (-LOG2E))
    cube = wide * wide * wide
    six = cube * cube
    twelve = six * six
    sharp = twelve * twelve
    wide = 0.08 * wide
    value = (wide + 0.1 * sharp) + t * (wide + 2.4 * sharp)
    slope = w * (wide + 57.6 * sharp)
    return value, slope


def box_corner(leaf):
    corner = []
    for axis in range(3):
        total = 0
        for bit in range(4):
            total = total + ((leaf >> (3 * bit + axis)) & 1) * (1 << bit)
        corner.append(total)
    return corner


def rows_of(corner, shape):
    row = lax.broadcasted_iota(jnp.int32, shape, 0)
    x, y, z = [jnp.asarray(c, jnp.int32).astype(f32) for c in corner]
    return jnp.where(row == 0, x, jnp.where(row == 1, y, jnp.where(row == 2, z, 0.0)))


def inside(index, count):
    return jnp.minimum(jnp.maximum(index, 0), count - 1)


def stacked(v):
    return jnp.concatenate([v[:, :SKEL], v[:, SKEL:]], axis=0)


def far_tile(columns, source):
    w = None
    for axis in range(3):
        gap = columns[axis] - source[axis : axis + 1, :]
        w = gap * gap if w is None else w + gap * gap
    value, slope = matern(w * (1.0 / 12.0))
    return jnp.concatenate([value, slope], axis=0)


def kernel(
    n_oct,
    n_leaf,
    probes_in,
    *refs,
):
    inputs, refs = refs[:12], refs[12:]
    outputs, refs = refs[:2], refs[2:]
    held, refs = refs[:12], refs[12:]
    run(n_oct, n_leaf, probes_in, inputs, held, *held, *outputs, *refs)


def run(
    n_oct,
    n_leaf,
    probes_in,
    inputs,
    held,
    offsets,
    basis,
    dev_transfer,
    oct_transfer,
    leaf_skel,
    dev_skel,
    oct_skel,
    near_list,
    near_count,
    leaf_far,
    dev_far,
    oct_far,
    out_value,
    out_slope,
    load_sem,
    pext,
    oext,
    wq,
    wsk,
    ag,
    tiles,
    gathered,
    regions,
    chosen,
    spread,
    feat_f,
    feat_g,
    kv0,
    ks0,
    kv1,
    ks1,
    acc,
    columns,
    far_sum,
    halo_send,
    halo_recv,
    ag_send,
    ag_recv,
    red_send,
    red_recv,
    oct_send,
    oct_recv,
    spread_send,
    spread_recv,
):
    o = lax.axis_index("oct")
    me = lax.axis_index("leaf")
    flat = o * n_leaf + me
    devices = n_oct * n_leaf
    right = lax.rem(flat + 1, devices)
    left = lax.rem(flat + devices - 1, devices)
    right_id = (right // n_leaf, lax.rem(right, n_leaf))
    left_id = (left // n_leaf, lax.rem(left, n_leaf))
    first = flat * LEAVES

    def in_region(k):
        return lax.rem(me + k, n_leaf)

    def across(k):
        return lax.rem(o + k, n_oct)

    loads = [
        pltpu.make_async_copy(
            probes_in.at[:, leaf * LEAF : (leaf + 1) * LEAF],
            pext.at[WIN + leaf],
            load_sem.at[leaf],
        )
        for leaf in range(LEAVES)
    ]
    loads += [
        pltpu.make_async_copy(source, target, load_sem.at[LEAVES + i])
        for i, (source, target) in enumerate(zip(inputs, held))
    ]
    for piece in loads:
        piece.start()

    barrier = pltpu.get_barrier_semaphore()

    def greet(device):
        pl.semaphore_signal(barrier, inc=1, device_id=device, device_id_type=MESH)

    greet(right_id)
    greet(left_id)

    def greet_region(k, _):
        greet((o, in_region(k)))
        return 0

    lax.fori_loop(1, n_leaf, greet_region, 0)

    def greet_across(k, _):
        greet((across(k), me))
        return 0

    lax.fori_loop(1, n_oct, greet_across, 0)

    for piece in loads:
        piece.wait()
    base = box_corner(first)
    row512 = lax.broadcasted_iota(jnp.int32, (LEAF, SKEL), 0)
    charges, picked, corners = [], [], []
    for leaf in range(LEAVES):
        span = slice(leaf * LEAF, (leaf + 1) * LEAF)
        own = jnp.concatenate([offsets[:, span].astype(f32), jnp.zeros((5, LEAF), f32)], axis=0)
        oext[WIN + leaf] = own
        one_hot = jnp.where(row512 == leaf_skel[leaf : leaf + 1, :], 1.0, 0.0).astype(bf16)
        picked.append(dot(own.astype(bf16), one_hot))
        corner = [base[0] + (leaf & 1), base[1] + (leaf >> 1 & 1), base[2] + (leaf >> 2 & 1)]
        corners.append(rows_of(corner, (8, SKEL)))
        wsk[LEAVES + leaf] = picked[-1] + corners[-1]
        charge = dot(pext[WIN + leaf], basis[leaf * SKEL : (leaf + 1) * SKEL, :], NT)
        charges.append(charge)
        wq[LEAVES + leaf] = jnp.concatenate(halves(charge), axis=1)
    q_dev = dot3(jnp.concatenate(charges, axis=1), dev_transfer[...], NT)
    upward = dot3(q_dev, oct_transfer[...], NT)
    both = jnp.concatenate(
        [jnp.concatenate(picked, axis=1), jnp.concatenate(corners, axis=1)], axis=0
    ).astype(bf16)
    one_hot = jnp.where(row512 == dev_skel[...], 1.0, 0.0).astype(bf16)
    dev_both = dot(both, one_hot)
    dev_pos = dev_both[:8] + dev_both[8:]
    ag[me] = jnp.concatenate(
        [q_dev, jnp.concatenate([dev_both, jnp.zeros((PROBES - 16, SKEL), f32)], axis=0)], axis=1
    ).astype(bf16)
    wanted = oct_skel[pl.ds(o, 1), :] - me * SKEL
    row64 = lax.broadcasted_iota(jnp.int32, (SKEL, SKEL), 0)
    one_hot = jnp.where(row64 == wanted, 1.0, 0.0).astype(bf16)
    oct_both = dot(dev_both.astype(bf16), one_hot)
    blank = jnp.zeros((8, SKEL), f32)
    for t in range(RED - 1):
        tiles[t] = jnp.concatenate([upward[8 * t : 8 * t + 8], blank], axis=1)
    tiles[RED - 1] = jnp.concatenate([oct_both[:8] + oct_both[8:], blank], axis=1)

    pl.semaphore_wait(barrier, n_leaf - 1 + n_oct - 1 + 2)

    def copy(src, dst, send, recv, device):
        return pltpu.make_async_remote_copy(
            src_ref=src,
            dst_ref=dst,
            send_sem=send,
            recv_sem=recv,
            device_id=device,
            device_id_type=MESH,
        )

    def reduce_copy(t, slot):
        return copy(
            tiles.at[t], gathered.at[slot], red_send.at[t], red_recv.at[slot], (o, t)
        )

    for t in range(RED):

        @pl.when(me != t)
        def _():
            reduce_copy(t, me).start()

    @pl.when(me < RED)
    def _():
        gathered[me] = tiles[me]

    own = slice(LEAVES, 2 * LEAVES)
    halo = [
        copy(pext.at[WIN : 2 * WIN], pext.at[WIN + LEAVES : EXT], halo_send.at[0], halo_recv.at[0], left_id),
        copy(oext.at[WIN : 2 * WIN], oext.at[WIN + LEAVES : EXT], halo_send.at[1], halo_recv.at[1], left_id),
        copy(pext.at[LEAVES : LEAVES + WIN], pext.at[0:WIN], halo_send.at[2], halo_recv.at[2], right_id),
        copy(oext.at[LEAVES : LEAVES + WIN], oext.at[0:WIN], halo_send.at[3], halo_recv.at[3], right_id),
        copy(wq.at[own], wq.at[2 * LEAVES : WIDE], halo_send.at[4], halo_recv.at[4], left_id),
        copy(wsk.at[own], wsk.at[2 * LEAVES : WIDE], halo_send.at[5], halo_recv.at[5], left_id),
        copy(wq.at[own], wq.at[0:LEAVES], halo_send.at[6], halo_recv.at[6], right_id),
        copy(wsk.at[own], wsk.at[0:LEAVES], halo_send.at[7], halo_recv.at[7], right_id),
    ]
    for piece in halo[:4]:
        piece.start()

    def gather_copy(peer, slot):
        return copy(ag.at[me], ag.at[slot], ag_send.at[peer], ag_recv.at[slot], (o, peer))

    def gather_start(k, _):
        gather_copy(in_region(k), me).start()
        return 0

    row8 = lax.broadcasted_iota(jnp.int32, (8, LEAF), 0)

    def features(e, corner):
        off = oext[e]
        anchor = rows_of(corner, (8, LEAF))
        pos = off + anchor
        norm = split3(jnp.sum(pos * pos, axis=0, keepdims=True) * (1.0 / 12.0))
        parts = split3(pos * (-1.0 / 6.0))

        def mixed(at):
            v = jnp.zeros((8, LEAF), f32)
            for i in range(3):
                v = jnp.where(row8 == at + i, norm[i], v)
            return jnp.where((row8 >= 3 - at) & (row8 < 6 - at), 1.0, v)

        pad = jnp.zeros((8, LEAF), f32)
        rows_f = jnp.concatenate([*parts, *parts, mixed(0), pad], axis=0)
        feat_f[e] = jnp.transpose(rows_f).astype(bf16)
        rows_g = jnp.concatenate([anchor] * 3 + [off] * 3 + [mixed(3), pad], axis=0)
        feat_g[e] = rows_g.astype(bf16)

    for leaf in range(LEAVES):
        features(WIN + leaf, [leaf & 1, leaf >> 1 & 1, leaf >> 2 & 1])
    for e in range(EXT):
        acc[e] = jnp.zeros((2, PROBES, LEAF), f32)

    def uses(target, source):
        leaf = lax.rem(target + LEAVES - WIN, LEAVES)
        wanted_leaf = first + source - WIN
        count = near_count[leaf]
        total = jnp.float32(0.0)
        for s in range(near_list.shape[1]):
            hit = (near_list[leaf, s] == wanted_leaf) & (s < count)
            total = total + jnp.where(hit, jnp.float32(1.0), jnp.float32(0.0))
        return total

    def tile(a, b, kv, ks, rows, cols):
        value, slope = matern(dot(feat_f[a, rows, :], feat_g[b, :, cols]))
        kv[rows, cols] = value.astype(bf16)
        ks[rows, cols] = slope.astype(bf16)

    def interleave(first_ops, second_ops):
        done = 0
        for i, op in enumerate(first_ops):
            op()
            upto = (i + 1) * len(second_ops) // len(first_ops)
            for q in range(done, upto):
                second_ops[q]()
            done = upto

    def pipe(n, make, use, between=lambda k: None):
        bufs = ((kv0, ks0), (kv1, ks1))
        for op in make(0, *bufs[0]):
            op()
        steps = (n - 1) // 2

        def body(k, _):
            between(k)
            interleave(make(2 * k + 1, *bufs[1]), use(2 * k, *bufs[0]))
            interleave(make(2 * k + 2, *bufs[0]), use(2 * k + 1, *bufs[1]))
            return 0

        lax.fori_loop(0, steps, body, 0)
        if n % 2:
            for op in use(n - 1, *bufs[0]):
                op()
        else:
            interleave(make(n - 1, *bufs[1]), use(n - 2, *bufs[0]))
            for op in use(n - 1, *bufs[1]):
                op()

    half = LEAF // 2
    low, high, full = slice(0, half), slice(half, LEAF), slice(0, LEAF)

    def self_make(i, kv, ks):
        e = i + WIN
        ops = []
        for r in range(0, LEAF, 64):
            cols = full if r < half else high
            ops.append(lambda r=r, cols=cols: tile(e, e, kv, ks, slice(r, r + 64), cols))
        return ops

    def self_use(i, kv, ks):
        e = i + WIN
        c = uses(e, e)
        ops = []
        for m, k in enumerate((kv, ks)):

            def upper(m=m, k=k):
                acc[e, m] = c * dot(pext[e, :, low], k[low, :])

            def corner(m=m, k=k):
                acc[e, m, :, high] += c * dot(pext[e, :, high], k[high, high])

            def lower(m=m, k=k):
                acc[e, m, :, low] += c * dot(pext[e, :, high], k[low, high], NT)

            ops += [upper, corner, lower]
        return ops

    def oct_copy(k, slot):
        return copy(
            tiles.at[0], regions.at[slot], oct_send.at[k], oct_recv.at[slot], (across(k), me)
        )

    def spread_copy(peer, slot):
        return copy(chosen, spread.at[slot], spread_send.at[peer], spread_recv.at[slot], (o, peer))

    def each(lo, hi, fn):
        def step(k, _):
            fn(k)
            return 0

        lax.fori_loop(lo, hi, step, 0)

    def sum_region():
        @pl.when(me < RED)
        def _():
            each(1, n_leaf, lambda k: reduce_copy(0, in_region(k)).wait_recv())
            for t in range(RED):

                @pl.when(me != t)
                def _():
                    reduce_copy(t, me).wait_send()

            total = jnp.sum(gathered[...], axis=0)
            regions[o] = total
            tiles[0] = total
            each(1, n_oct, lambda k: oct_copy(k, o).start())

    def spread_regions():
        @pl.when(me < RED)
        def _():
            each(1, n_oct, lambda k: oct_copy(k, across(k)).wait_recv())
            one, two = [regions[inside(oct_far[0, i], n_oct)] for i in range(2)]
            pair_of = jnp.concatenate([one[:, :SKEL], two[:, :SKEL]], axis=1)
            mine = jnp.concatenate([regions[o][:3], regions[o][:3], regions[o][:2]], axis=0)
            row = lax.broadcasted_iota(jnp.int32, (8, 2 * SKEL), 0)
            message = jnp.where((row >= 3) & (me == RED - 1), mine, pair_of)
            chosen[...] = message
            spread[me] = message
            each(1, n_leaf, lambda k: spread_copy(in_region(k), me).start())

        for piece in halo[4:]:
            piece.start()
        lax.fori_loop(1, n_leaf, gather_start, 0)

    def between_self(k):
        pl.when(k == 2)(sum_region)

    pipe(LEAVES, self_make, self_use, between_self)

    for piece in halo[:4]:
        piece.wait_recv()
    for e in list(range(WIN)) + list(range(WIN + LEAVES, EXT)):
        leaf = lax.rem(first + devices * LEAVES + e - WIN, devices * LEAVES)
        there = box_corner(leaf)
        features(e, [there[i] - base[i] for i in range(3)])

    def pair(i):
        s = (i + 1) // 10
        a = i + 1 - 10 * s
        return a, a + 1 + s

    def pair_make(i, kv, ks):
        a, b = pair(i)
        return [
            lambda r=r: tile(a, b, kv, ks, slice(r, r + 64), full) for r in range(0, LEAF, 64)
        ]

    def pair_use(i, kv, ks):
        a, b = pair(i)
        to_b = uses(b, a)
        to_a = uses(a, b)
        ops = []
        for m, k in enumerate((kv, ks)):
            for span in (low, high):

                def forward(m=m, k=k, span=span):
                    acc[b, m, :, span] += to_b * dot(pext[a], k[:, span])

                def back(m=m, k=k, span=span):
                    acc[a, m, :, span] += to_a * dot(pext[b], k[span, :], NT)

                ops += [forward, back]
        return ops

    def between(k):
        pl.when(k == 2)(spread_regions)

    pipe(19, pair_make, pair_use, between)

    upright = jnp.concatenate(
        [wsk[LEAVES + leaf] for leaf in range(LEAVES)] + [dev_pos] + [blank] * 7, axis=0
    )
    upright = jnp.transpose(upright)
    wide = (SKEL, 2 * SKEL)
    for leaf in range(LEAVES + 1):
        for axis in range(3):
            at = 8 * leaf + axis
            columns[leaf, axis] = jnp.broadcast_to(upright[:, at : at + 1], wide)

    for piece in halo[4:]:
        piece.wait_recv()

    def leaf_field(leaf, _):
        targets = [columns[leaf, axis] for axis in range(3)]
        total = jnp.zeros(wide, f32)
        for pairing in range(2):
            x = inside(leaf_far[leaf, 2 * pairing] - first + LEAVES, WIDE)
            y = inside(leaf_far[leaf, 2 * pairing + 1] - first + LEAVES, WIDE)
            source = jnp.concatenate([wsk[x], wsk[y]], axis=1)
            one, two = wq[x], wq[y]
            high = jnp.concatenate([one[:, :SKEL], two[:, :SKEL]], axis=1)
            rest = jnp.concatenate([one[:, SKEL:], two[:, SKEL:]], axis=1)
            tile_high, tile_rest = halves(far_tile(targets, source))
            total += dot(high, tile_high, NT) + (dot(rest, tile_high, NT) + dot(high, tile_rest, NT))
        far_sum[leaf] = total
        return 0

    lax.fori_loop(0, LEAVES, leaf_field, 0)

    each(1, n_leaf, lambda k: gather_copy(me, in_region(k)).wait_recv())
    targets = [columns[LEAVES, axis] for axis in range(3)]
    dev_sum = jnp.zeros(wide, f32)
    for pairing in range(2):
        pieces = [
            ag[inside(dev_far[0, 2 * pairing + i] - o * n_leaf, n_leaf)].astype(f32)
            for i in range(2)
        ]
        source = jnp.concatenate([v[:8, SKEL:] + v[8:16, SKEL:] for v in pieces], axis=1)
        charge = jnp.concatenate([v[:, :SKEL] for v in pieces], axis=1)
        dev_sum += dot3(charge, far_tile(targets, source), NT)

    for t in range(RED):

        @pl.when(me != t)
        def _():
            spread_copy(t, t).wait_recv()

    charge = spread[0 : RED - 1].reshape(PROBES, 2 * SKEL)
    source = spread[RED - 1]
    upright = jnp.transpose(
        jnp.concatenate([source, jnp.zeros((120, 2 * SKEL), f32)], axis=0)
    )
    targets = [upright[:SKEL, 3 + axis : 4 + axis] for axis in range(3)]
    oct_sum = dot3(charge, far_tile(targets, source), NT)
    down_dev = dot3(stacked(oct_sum), oct_transfer[...]) + stacked(dev_sum)
    down = dot3(down_dev, dev_transfer[...])
    for leaf in range(LEAVES):
        span = slice(leaf * LEAF, (leaf + 1) * LEAF)
        cols = slice(leaf * SKEL, (leaf + 1) * SKEL)
        mine = (down[:, cols] + stacked(far_sum[leaf])).astype(bf16)
        field = dot(mine, basis[cols, :])
        out_value[:, span] = acc[WIN + leaf, 0] + field[:PROBES]
        out_slope[:, span] = acc[WIN + leaf, 1] + field[PROBES:]

    for piece in halo:
        piece.wait_send()
    each(1, n_leaf, lambda k: gather_copy(in_region(k), me).wait_send())

    @pl.when(me < RED)
    def _():
        each(1, n_oct, lambda k: oct_copy(k, o).wait_send())
        each(1, n_leaf, lambda k: spread_copy(in_region(k), me).wait_send())

    @pl.when(me >= RED)
    def _():
        for t in range(RED):
            reduce_copy(t, me).wait_send()


def body(n_oct, n_leaf, *args):
    (
        probes,
        offsets,
        leaf_basis,
        dev_transfer,
        oct_transfer,
        near_list,
        near_count,
        leaf_far,
        dev_far,
        oct_far,
        leaf_skel,
        dev_skel,
        oct_skel,
    ) = args
    vmem = pl.BlockSpec(memory_space=pltpu.VMEM)
    hbm = pl.BlockSpec(memory_space=pltpu.HBM)
    points = probes.shape[1]
    in_vmem = (
        offsets,
        leaf_basis,
        dev_transfer,
        oct_transfer,
        leaf_skel,
        dev_skel,
        oct_skel,
    )
    in_smem = (near_list, near_count, leaf_far, dev_far, oct_far)
    dma = pltpu.SemaphoreType.DMA
    out = jax.ShapeDtypeStruct((PROBES, points), f32)
    return pl.pallas_call(
        functools.partial(kernel, n_oct, n_leaf),
        out_shape=(out, out),
        in_specs=[hbm] * 13,
        out_specs=(vmem, vmem),
        scratch_shapes=[
            *[pltpu.VMEM(v.shape, v.dtype) for v in in_vmem],
            *[pltpu.SMEM(v.shape, v.dtype) for v in in_smem],
            dma((LEAVES + 12,)),
            pltpu.VMEM((EXT, PROBES, LEAF), bf16),
            pltpu.VMEM((EXT, 8, LEAF), f32),
            pltpu.VMEM((WIDE, PROBES, 2 * SKEL), bf16),
            pltpu.VMEM((WIDE, 8, SKEL), f32),
            pltpu.VMEM((n_leaf, PROBES, 2 * SKEL), bf16),
            pltpu.VMEM((RED, 8, 2 * SKEL), f32),
            pltpu.VMEM((n_leaf, 8, 2 * SKEL), f32),
            pltpu.VMEM((n_oct, 8, 2 * SKEL), f32),
            pltpu.VMEM((8, 2 * SKEL), f32),
            pltpu.VMEM((RED, 8, 2 * SKEL), f32),
            pltpu.VMEM((EXT, LEAF, FEAT), bf16),
            pltpu.VMEM((EXT, FEAT, LEAF), bf16),
            pltpu.VMEM((LEAF, LEAF), bf16),
            pltpu.VMEM((LEAF, LEAF), bf16),
            pltpu.VMEM((LEAF, LEAF), bf16),
            pltpu.VMEM((LEAF, LEAF), bf16),
            pltpu.VMEM((EXT, 2, PROBES, LEAF), f32),
            pltpu.VMEM((LEAVES + 1, 3, SKEL, 2 * SKEL), f32),
            pltpu.VMEM((LEAVES, PROBES, 2 * SKEL), f32),
            dma((8,)),
            dma((8,)),
            dma((n_leaf,)),
            dma((n_leaf,)),
            dma((RED,)),
            dma((n_leaf,)),
            dma((n_oct,)),
            dma((n_oct,)),
            dma((n_leaf,)),
            dma((n_leaf,)),
        ],
        compiler_params=pltpu.CompilerParams(
            collective_id=0, has_side_effects=True, vmem_limit_bytes=60 * 2**20
        ),
    )(probes, *in_vmem, *in_smem)


def solution(mesh):
    return jax.shard_map(
        functools.partial(body, mesh.shape["oct"], mesh.shape["leaf"]),
        mesh=mesh,
        in_specs=(
            P(None, ("oct", "leaf")),
            P(None, ("oct", "leaf")),
            P(("oct", "leaf"), None),
            P(("oct", "leaf"), None),
            P(("oct", "leaf"), None),
            P(("oct", "leaf"), None),
            P(("oct", "leaf")),
            P(("oct", "leaf"), None),
            P(("oct", "leaf"), None),
            P("oct", None),
            P(("oct", "leaf"), None),
            P(("oct", "leaf"), None),
            P(),
        ),
        out_specs=(P(None, ("oct", "leaf")), P(None, ("oct", "leaf"))),
        check_vma=False,
    )
```

```python
import functools
import math

import jax
import jax.numpy as jnp
from jax import lax
from jax.experimental import pallas as pl
from jax.experimental.pallas import tpu as pltpu
from jax.sharding import PartitionSpec as P

LEAF = 512
SKEL = 64
PROBES = 64
LEAVES = 8
WIN = 2
EXT = LEAVES + 2 * WIN
WIDE = 3 * LEAVES
RED = 9
FEAT = 64

MESH = pl.DeviceIdType.MESH
f32 = jnp.float32
bf16 = jnp.bfloat16
LOG2E = math.log2(math.e)
NN = (((1,), (0,)), ((), ()))
NT = (((1,), (1,)), ((), ()))


def dot(a, b, dims=NN):
    return lax.dot_general(a, b, dims, preferred_element_type=f32)


def halves(v):
    high = v.astype(bf16)
    return high, (v - high.astype(f32)).astype(bf16)


def dot3(a, b, dims=NN):
    ah, al = halves(a)
    bh, bl = halves(b)
    return dot(ah, bh, dims) + (dot(ah, bl, dims) + dot(al, bh, dims))


def split3(v):
    high = v.astype(bf16).astype(f32)
    rest = v - high
    mid = rest.astype(bf16).astype(f32)
    return high, mid, (rest - mid).astype(bf16).astype(f32)


def matern(w):
    w = jnp.maximum(w, 1e-30)
    t = w * lax.rsqrt(w)
    wide = jnp.exp2(t * (-LOG2E))
    cube = wide * wide * wide
    six = cube * cube
    twelve = six * six
    sharp = twelve * twelve
    wide = 0.08 * wide
    value = (wide + 0.1 * sharp) + t * (wide + 2.4 * sharp)
    slope = w * (wide + 57.6 * sharp)
    return value, slope


def box_corner(leaf):
    corner = []
    for axis in range(3):
        total = 0
        for bit in range(4):
            total = total + ((leaf >> (3 * bit + axis)) & 1) * (1 << bit)
        corner.append(total)
    return corner


def rows_of(corner, shape):
    row = lax.broadcasted_iota(jnp.int32, shape, 0)
    x, y, z = [jnp.asarray(c, jnp.int32).astype(f32) for c in corner]
    return jnp.where(row == 0, x, jnp.where(row == 1, y, jnp.where(row == 2, z, 0.0)))


def inside(index, count):
    return jnp.minimum(jnp.maximum(index, 0), count - 1)


def stacked(v):
    return jnp.concatenate([v[:, :SKEL], v[:, SKEL:]], axis=0)


def far_tile(columns, source):
    w = None
    for axis in range(3):
        gap = columns[axis] - source[axis : axis + 1, :]
        w = gap * gap if w is None else w + gap * gap
    value, slope = matern(w * (1.0 / 12.0))
    return jnp.concatenate([value, slope], axis=0)


def kernel(
    n_oct,
    n_leaf,
    probes_in,
    *refs,
):
    inputs, refs = refs[:12], refs[12:]
    outputs, refs = refs[:2], refs[2:]
    held, refs = refs[:12], refs[12:]
    run(n_oct, n_leaf, probes_in, inputs, held, *held, *outputs, *refs)


def run(
    n_oct,
    n_leaf,
    probes_in,
    inputs,
    held,
    offsets,
    basis,
    dev_transfer,
    oct_transfer,
    leaf_skel,
    dev_skel,
    oct_skel,
    near_list,
    near_count,
    leaf_far,
    dev_far,
    oct_far,
    out_value,
    out_slope,
    load_sem,
    pext,
    oext,
    wq,
    wsk,
    ag,
    tiles,
    gathered,
    regions,
    chosen,
    spread,
    feat_f,
    feat_g,
    kv0,
    ks0,
    kv1,
    ks1,
    acc,
    columns,
    far_sum,
    halo_send,
    halo_recv,
    ag_send,
    ag_recv,
    red_send,
    red_recv,
    oct_send,
    oct_recv,
    spread_send,
    spread_recv,
):
    o = lax.axis_index("oct")
    me = lax.axis_index("leaf")
    flat = o * n_leaf + me
    devices = n_oct * n_leaf
    right = lax.rem(flat + 1, devices)
    left = lax.rem(flat + devices - 1, devices)
    right_id = (right // n_leaf, lax.rem(right, n_leaf))
    left_id = (left // n_leaf, lax.rem(left, n_leaf))
    first = flat * LEAVES

    def in_region(k):
        return lax.rem(me + k, n_leaf)

    def across(k):
        return lax.rem(o + k, n_oct)

    loads = [
        pltpu.make_async_copy(
            probes_in.at[:, leaf * LEAF : (leaf + 1) * LEAF],
            pext.at[WIN + leaf],
            load_sem.at[leaf],
        )
        for leaf in range(LEAVES)
    ]
    loads += [
        pltpu.make_async_copy(source, target, load_sem.at[LEAVES + i])
        for i, (source, target) in enumerate(zip(inputs, held))
    ]
    for piece in loads:
        piece.start()

    barrier = pltpu.get_barrier_semaphore()

    def greet(device):
        pl.semaphore_signal(barrier, inc=1, device_id=device, device_id_type=MESH)

    greet(right_id)
    greet(left_id)

    def greet_region(k, _):
        greet((o, in_region(k)))
        return 0

    lax.fori_loop(1, n_leaf, greet_region, 0)

    def greet_across(k, _):
        greet((across(k), me))
        return 0

    lax.fori_loop(1, n_oct, greet_across, 0)

    for piece in loads:
        piece.wait()
    base = box_corner(first)
    row512 = lax.broadcasted_iota(jnp.int32, (LEAF, SKEL), 0)
    charges, picked, corners = [], [], []
    for leaf in range(LEAVES):
        span = slice(leaf * LEAF, (leaf + 1) * LEAF)
        own = jnp.concatenate([offsets[:, span].astype(f32), jnp.zeros((5, LEAF), f32)], axis=0)
        oext[WIN + leaf] = own
        one_hot = jnp.where(row512 == leaf_skel[leaf : leaf + 1, :], 1.0, 0.0).astype(bf16)
        picked.append(dot(own.astype(bf16), one_hot))
        corner = [base[0] + (leaf & 1), base[1] + (leaf >> 1 & 1), base[2] + (leaf >> 2 & 1)]
        corners.append(rows_of(corner, (8, SKEL)))
        wsk[LEAVES + leaf] = picked[-1] + corners[-1]
        charge = dot(pext[WIN + leaf], basis[leaf * SKEL : (leaf + 1) * SKEL, :], NT)
        charges.append(charge)
        wq[LEAVES + leaf] = jnp.concatenate(halves(charge), axis=1)
    q_dev = dot3(jnp.concatenate(charges, axis=1), dev_transfer[...], NT)
    upward = dot3(q_dev, oct_transfer[...], NT)
    both = jnp.concatenate(
        [jnp.concatenate(picked, axis=1), jnp.concatenate(corners, axis=1)], axis=0
    ).astype(bf16)
    one_hot = jnp.where(row512 == dev_skel[...], 1.0, 0.0).astype(bf16)
    dev_both = dot(both, one_hot)
    dev_pos = dev_both[:8] + dev_both[8:]
    ag[me] = jnp.concatenate(
        [q_dev, jnp.concatenate([dev_both, jnp.zeros((PROBES - 16, SKEL), f32)], axis=0)], axis=1
    ).astype(bf16)
    wanted = oct_skel[pl.ds(o, 1), :] - me * SKEL
    row64 = lax.broadcasted_iota(jnp.int32, (SKEL, SKEL), 0)
    one_hot = jnp.where(row64 == wanted, 1.0, 0.0).astype(bf16)
    oct_both = dot(dev_both.astype(bf16), one_hot)
    blank = jnp.zeros((8, SKEL), f32)
    for t in range(RED - 1):
        tiles[t] = jnp.concatenate([upward[8 * t : 8 * t + 8], blank], axis=1)
    tiles[RED - 1] = jnp.concatenate([oct_both[:8] + oct_both[8:], blank], axis=1)

    row8 = lax.broadcasted_iota(jnp.int32, (8, LEAF), 0)

    def features(e, corner):
        off = oext[e]
        anchor = rows_of(corner, (8, LEAF))
        pos = off + anchor
        norm = split3(jnp.sum(pos * pos, axis=0, keepdims=True) * (1.0 / 12.0))
        parts = split3(pos * (-1.0 / 6.0))

        def mixed(at):
            v = jnp.zeros((8, LEAF), f32)
            for i in range(3):
                v = jnp.where(row8 == at + i, norm[i], v)
            return jnp.where((row8 >= 3 - at) & (row8 < 6 - at), 1.0, v)

        pad = jnp.zeros((8, LEAF), f32)
        rows_f = jnp.concatenate([*parts, *parts, mixed(0), pad], axis=0)
        feat_f[e] = jnp.transpose(rows_f).astype(bf16)
        rows_g = jnp.concatenate([anchor] * 3 + [off] * 3 + [mixed(3), pad], axis=0)
        feat_g[e] = rows_g.astype(bf16)

    for leaf in range(LEAVES):
        features(WIN + leaf, [leaf & 1, leaf >> 1 & 1, leaf >> 2 & 1])

    def uses(target, source):
        leaf = lax.rem(target + LEAVES - WIN, LEAVES)
        wanted_leaf = first + source - WIN
        count = near_count[leaf]
        total = jnp.float32(0.0)
        for s in range(near_list.shape[1]):
            hit = (near_list[leaf, s] == wanted_leaf) & (s < count)
            total = total + jnp.where(hit, jnp.float32(1.0), jnp.float32(0.0))
        return total

    def tile(a, b, kv, ks, rows, cols):
        value, slope = matern(dot(feat_f[a, rows, :], feat_g[b, :, cols]))
        kv[rows, cols] = value.astype(bf16)
        ks[rows, cols] = slope.astype(bf16)

    def interleave(first_ops, second_ops):
        done = 0
        for i, op in enumerate(first_ops):
            op()
            upto = (i + 1) * len(second_ops) // len(first_ops)
            for q in range(done, upto):
                second_ops[q]()
            done = upto

    def pipe(n, make, use, between=lambda k: None):
        bufs = ((kv0, ks0), (kv1, ks1))
        for op in make(0, *bufs[0]):
            op()
        steps = (n - 1) // 2

        def body(k, _):
            between(k)
            interleave(make(2 * k + 1, *bufs[1]), use(2 * k, *bufs[0]))
            interleave(make(2 * k + 2, *bufs[0]), use(2 * k + 1, *bufs[1]))
            return 0

        lax.fori_loop(0, steps, body, 0)
        if n % 2:
            for op in use(n - 1, *bufs[0]):
                op()
        else:
            interleave(make(n - 1, *bufs[1]), use(n - 2, *bufs[0]))
            for op in use(n - 1, *bufs[1]):
                op()

    half = LEAF // 2
    low, high, full = slice(0, half), slice(half, LEAF), slice(0, LEAF)

    def self_make(i, kv, ks):
        e = i + WIN
        ops = []
        for r in range(0, LEAF, 64):
            cols = full if r < half else high
            ops.append(lambda r=r, cols=cols: tile(e, e, kv, ks, slice(r, r + 64), cols))
        return ops

    def self_use(i, kv, ks):
        e = i + WIN
        c = uses(e, e)
        ops = []
        for m, k in enumerate((kv, ks)):

            def upper(m=m, k=k):
                acc[e, m] = c * dot(pext[e, :, low], k[low, :])

            def corner(m=m, k=k):
                acc[e, m, :, high] += c * dot(pext[e, :, high], k[high, high])

            def lower(m=m, k=k):
                acc[e, m, :, low] += c * dot(pext[e, :, high], k[low, high], NT)

            ops += [upper, corner, lower]
        return ops

    pipe(LEAVES, self_make, self_use)

    pl.semaphore_wait(barrier, n_leaf - 1 + n_oct - 1 + 2)

    def copy(src, dst, send, recv, device):
        return pltpu.make_async_remote_copy(
            src_ref=src,
            dst_ref=dst,
            send_sem=send,
            recv_sem=recv,
            device_id=device,
            device_id_type=MESH,
        )

    def reduce_copy(t, slot):
        return copy(
            tiles.at[t], gathered.at[slot], red_send.at[t], red_recv.at[slot], (o, t)
        )

    for t in range(RED):

        @pl.when(me != t)
        def _():
            reduce_copy(t, me).start()

    @pl.when(me < RED)
    def _():
        gathered[me] = tiles[me]

    own = slice(LEAVES, 2 * LEAVES)
    halo = [
        copy(pext.at[WIN : 2 * WIN], pext.at[WIN + LEAVES : EXT], halo_send.at[0], halo_recv.at[0], left_id),
        copy(oext.at[WIN : 2 * WIN], oext.at[WIN + LEAVES : EXT], halo_send.at[1], halo_recv.at[1], left_id),
        copy(pext.at[LEAVES : LEAVES + WIN], pext.at[0:WIN], halo_send.at[2], halo_recv.at[2], right_id),
        copy(oext.at[LEAVES : LEAVES + WIN], oext.at[0:WIN], halo_send.at[3], halo_recv.at[3], right_id),
        copy(wq.at[own], wq.at[2 * LEAVES : WIDE], halo_send.at[4], halo_recv.at[4], left_id),
        copy(wsk.at[own], wsk.at[2 * LEAVES : WIDE], halo_send.at[5], halo_recv.at[5], left_id),
        copy(wq.at[own], wq.at[0:LEAVES], halo_send.at[6], halo_recv.at[6], right_id),
        copy(wsk.at[own], wsk.at[0:LEAVES], halo_send.at[7], halo_recv.at[7], right_id),
    ]
    for piece in halo[:4]:
        piece.start()

    def gather_copy(peer, slot):
        return copy(ag.at[me], ag.at[slot], ag_send.at[peer], ag_recv.at[slot], (o, peer))

    def gather_start(k, _):
        gather_copy(in_region(k), me).start()
        return 0


    def oct_copy(k, slot):
        return copy(
            tiles.at[0], regions.at[slot], oct_send.at[k], oct_recv.at[slot], (across(k), me)
        )

    def spread_copy(peer, slot):
        return copy(chosen, spread.at[slot], spread_send.at[peer], spread_recv.at[slot], (o, peer))

    def each(lo, hi, fn):
        def step(k, _):
            fn(k)
            return 0

        lax.fori_loop(lo, hi, step, 0)

    def sum_region():
        @pl.when(me < RED)
        def _():
            each(1, n_leaf, lambda k: reduce_copy(0, in_region(k)).wait_recv())
            for t in range(RED):

                @pl.when(me != t)
                def _():
                    reduce_copy(t, me).wait_send()

            total = jnp.sum(gathered[...], axis=0)
            regions[o] = total
            tiles[0] = total
            each(1, n_oct, lambda k: oct_copy(k, o).start())

    def spread_regions():
        @pl.when(me < RED)
        def _():
            each(1, n_oct, lambda k: oct_copy(k, across(k)).wait_recv())
            one, two = [regions[inside(oct_far[0, i], n_oct)] for i in range(2)]
            pair_of = jnp.concatenate([one[:, :SKEL], two[:, :SKEL]], axis=1)
            mine = jnp.concatenate([regions[o][:3], regions[o][:3], regions[o][:2]], axis=0)
            row = lax.broadcasted_iota(jnp.int32, (8, 2 * SKEL), 0)
            message = jnp.where((row >= 3) & (me == RED - 1), mine, pair_of)
            chosen[...] = message
            spread[me] = message
            each(1, n_leaf, lambda k: spread_copy(in_region(k), me).start())


    def pair(i):
        s = i // 7
        a = i + WIN - 7 * s
        return a, a + 1 + s

    def pair_make(i, kv, ks):
        a, b = pair(i)
        return [
            lambda r=r: tile(a, b, kv, ks, slice(r, r + 64), full) for r in range(0, LEAF, 64)
        ]

    def pair_use(i, kv, ks):
        a, b = pair(i)
        to_b = uses(b, a)
        to_a = uses(a, b)
        ops = []
        for m, k in enumerate((kv, ks)):
            for span in (low, high):

                def forward(m=m, k=k, span=span):
                    acc[b, m, :, span] += to_b * dot(pext[a], k[:, span])

                def back(m=m, k=k, span=span):
                    acc[a, m, :, span] += to_a * dot(pext[b], k[span, :], NT)

                ops += [forward, back]
        return ops

    def bulk():
        for piece in halo[4:]:
            piece.start()
        lax.fori_loop(1, n_leaf, gather_start, 0)

    def between(k):
        pl.when(k == 2)(sum_region)
        pl.when(k == 2)(bulk)
        pl.when(k == 4)(spread_regions)

    pipe(13, pair_make, pair_use, between)

    for piece in halo[:4]:
        piece.wait_recv()
    for e in list(range(WIN)) + list(range(WIN + LEAVES, EXT)):
        leaf = lax.rem(first + devices * LEAVES + e - WIN, devices * LEAVES)
        there = box_corner(leaf)
        features(e, [there[i] - base[i] for i in range(3)])

    def edge(i):
        r = i % 3
        source, target = 1 - r % 2, 2 + r // 2
        side = i // 3
        last = EXT - 1
        return source + side * (last - 2 * source), target + side * (last - 2 * target)

    def edge_make(i, kv, ks):
        a, b = edge(i)
        return [
            lambda r=r: tile(a, b, kv, ks, slice(r, r + 64), full) for r in range(0, LEAF, 64)
        ]

    def edge_use(i, kv, ks):
        a, b = edge(i)
        c = uses(b, a)
        ops = []
        for m, k in enumerate((kv, ks)):
            for span in (low, high):

                def forward(m=m, k=k, span=span):
                    acc[b, m, :, span] += c * dot(pext[a], k[:, span])

                ops.append(forward)
        return ops

    pipe(6, edge_make, edge_use)

    upright = jnp.concatenate(
        [wsk[LEAVES + leaf] for leaf in range(LEAVES)] + [dev_pos] + [blank] * 7, axis=0
    )
    upright = jnp.transpose(upright)
    wide = (SKEL, 2 * SKEL)
    for leaf in range(LEAVES + 1):
        for axis in range(3):
            at = 8 * leaf + axis
            columns[leaf, axis] = jnp.broadcast_to(upright[:, at : at + 1], wide)

    for piece in halo[4:]:
        piece.wait_recv()

    def leaf_field(leaf, _):
        targets = [columns[leaf, axis] for axis in range(3)]
        total = jnp.zeros(wide, f32)
        for pairing in range(2):
            x = inside(leaf_far[leaf, 2 * pairing] - first + LEAVES, WIDE)
            y = inside(leaf_far[leaf, 2 * pairing + 1] - first + LEAVES, WIDE)
            source = jnp.concatenate([wsk[x], wsk[y]], axis=1)
            one, two = wq[x], wq[y]
            high = jnp.concatenate([one[:, :SKEL], two[:, :SKEL]], axis=1)
            rest = jnp.concatenate([one[:, SKEL:], two[:, SKEL:]], axis=1)
            tile_high, tile_rest = halves(far_tile(targets, source))
            total += dot(high, tile_high, NT) + (dot(rest, tile_high, NT) + dot(high, tile_rest, NT))
        far_sum[leaf] = total
        return 0

    lax.fori_loop(0, LEAVES, leaf_field, 0, unroll=4)

    each(1, n_leaf, lambda k: gather_copy(me, in_region(k)).wait_recv())
    targets = [columns[LEAVES, axis] for axis in range(3)]
    dev_sum = jnp.zeros(wide, f32)
    for pairing in range(2):
        pieces = [
            ag[inside(dev_far[0, 2 * pairing + i] - o * n_leaf, n_leaf)].astype(f32)
            for i in range(2)
        ]
        source = jnp.concatenate([v[:8, SKEL:] + v[8:16, SKEL:] for v in pieces], axis=1)
        charge = jnp.concatenate([v[:, :SKEL] for v in pieces], axis=1)
        dev_sum += dot3(charge, far_tile(targets, source), NT)

    for t in range(RED):

        @pl.when(me != t)
        def _():
            spread_copy(t, t).wait_recv()

    charge = spread[0 : RED - 1].reshape(PROBES, 2 * SKEL)
    source = spread[RED - 1]
    upright = jnp.transpose(
        jnp.concatenate([source, jnp.zeros((120, 2 * SKEL), f32)], axis=0)
    )
    targets = [upright[:SKEL, 3 + axis : 4 + axis] for axis in range(3)]
    oct_sum = dot3(charge, far_tile(targets, source), NT)
    down_dev = dot3(stacked(oct_sum), oct_transfer[...]) + stacked(dev_sum)
    down = dot3(down_dev, dev_transfer[...])
    for leaf in range(LEAVES):
        span = slice(leaf * LEAF, (leaf + 1) * LEAF)
        cols = slice(leaf * SKEL, (leaf + 1) * SKEL)
        mine = (down[:, cols] + stacked(far_sum[leaf])).astype(bf16)
        field = dot(mine, basis[cols, :])
        out_value[:, span] = acc[WIN + leaf, 0] + field[:PROBES]
        out_slope[:, span] = acc[WIN + leaf, 1] + field[PROBES:]

    for piece in halo:
        piece.wait_send()
    each(1, n_leaf, lambda k: gather_copy(in_region(k), me).wait_send())

    @pl.when(me < RED)
    def _():
        each(1, n_oct, lambda k: oct_copy(k, o).wait_send())
        each(1, n_leaf, lambda k: spread_copy(in_region(k), me).wait_send())

    @pl.when(me >= RED)
    def _():
        for t in range(RED):
            reduce_copy(t, me).wait_send()


def body(n_oct, n_leaf, *args):
    (
        probes,
        offsets,
        leaf_basis,
        dev_transfer,
        oct_transfer,
        near_list,
        near_count,
        leaf_far,
        dev_far,
        oct_far,
        leaf_skel,
        dev_skel,
        oct_skel,
    ) = args
    vmem = pl.BlockSpec(memory_space=pltpu.VMEM)
    hbm = pl.BlockSpec(memory_space=pltpu.HBM)
    points = probes.shape[1]
    in_vmem = (
        offsets,
        leaf_basis,
        dev_transfer,
        oct_transfer,
        leaf_skel,
        dev_skel,
        oct_skel,
    )
    in_smem = (near_list, near_count, leaf_far, dev_far, oct_far)
    dma = pltpu.SemaphoreType.DMA
    out = jax.ShapeDtypeStruct((PROBES, points), f32)
    return pl.pallas_call(
        functools.partial(kernel, n_oct, n_leaf),
        out_shape=(out, out),
        in_specs=[hbm] * 13,
        out_specs=(vmem, vmem),
        scratch_shapes=[
            *[pltpu.VMEM(v.shape, v.dtype) for v in in_vmem],
            *[pltpu.SMEM(v.shape, v.dtype) for v in in_smem],
            dma((LEAVES + 12,)),
            pltpu.VMEM((EXT, PROBES, LEAF), bf16),
            pltpu.VMEM((EXT, 8, LEAF), f32),
            pltpu.VMEM((WIDE, PROBES, 2 * SKEL), bf16),
            pltpu.VMEM((WIDE, 8, SKEL), f32),
            pltpu.VMEM((n_leaf, PROBES, 2 * SKEL), bf16),
            pltpu.VMEM((RED, 8, 2 * SKEL), f32),
            pltpu.VMEM((n_leaf, 8, 2 * SKEL), f32),
            pltpu.VMEM((n_oct, 8, 2 * SKEL), f32),
            pltpu.VMEM((8, 2 * SKEL), f32),
            pltpu.VMEM((RED, 8, 2 * SKEL), f32),
            pltpu.VMEM((EXT, LEAF, FEAT), bf16),
            pltpu.VMEM((EXT, FEAT, LEAF), bf16),
            pltpu.VMEM((LEAF, LEAF), bf16),
            pltpu.VMEM((LEAF, LEAF), bf16),
            pltpu.VMEM((LEAF, LEAF), bf16),
            pltpu.VMEM((LEAF, LEAF), bf16),
            pltpu.VMEM((EXT, 2, PROBES, LEAF), f32),
            pltpu.VMEM((LEAVES + 1, 3, SKEL, 2 * SKEL), f32),
            pltpu.VMEM((LEAVES, PROBES, 2 * SKEL), f32),
            dma((8,)),
            dma((8,)),
            dma((n_leaf,)),
            dma((n_leaf,)),
            dma((RED,)),
            dma((n_leaf,)),
            dma((n_oct,)),
            dma((n_oct,)),
            dma((n_leaf,)),
            dma((n_leaf,)),
        ],
        compiler_params=pltpu.CompilerParams(
            collective_id=0, has_side_effects=True, vmem_limit_bytes=60 * 2**20
        ),
    )(probes, *in_vmem, *in_smem)


def solution(mesh):
    return jax.shard_map(
        functools.partial(body, mesh.shape["oct"], mesh.shape["leaf"]),
        mesh=mesh,
        in_specs=(
            P(None, ("oct", "leaf")),
            P(None, ("oct", "leaf")),
            P(("oct", "leaf"), None),
            P(("oct", "leaf"), None),
            P(("oct", "leaf"), None),
            P(("oct", "leaf"), None),
            P(("oct", "leaf")),
            P(("oct", "leaf"), None),
            P(("oct", "leaf"), None),
            P("oct", None),
            P(("oct", "leaf"), None),
            P(("oct", "leaf"), None),
            P(),
        ),
        out_specs=(P(None, ("oct", "leaf")), P(None, ("oct", "leaf"))),
        check_vma=False,
    )
```
